256 devices in a mesh: grp: 8 (over x, core), rep: 32 (over z, y).
Axes of the slice: x: 4, y: 4, z: 8, core: 2. Of those that a mesh axis runs over, the one named last changes fastest.
Arguments:
- hidden: bfloat16 [131072, 3328], P(('grp', 'rep')), may hold values from -6 to 6
- out_grad: bfloat16 [131072, 2048], P(('grp', 'rep')), may hold values from -0.09375 to 0.09375
- error_in: bfloat16 [32, 2048, 3328], P('rep', 'grp'), may hold values from -6 to 6
- initial_basis: bfloat16 [16, 3328, 64], P('grp'), may hold values from -0.109375 to 0.109375
- block_ranks: int32 [16], P('grp'), may hold values from 8 to 64, as said below
Outputs:
- new_error: float32 [32, 2048, 3328], P('rep', 'grp')
- next_basis: float32 [16, 3328, 64], P('grp')
The draws below stay inside these ranges and needn't reach their ends.
Inputs may be any that keep to these rules, and one draw needn't show every extreme that they name: `block_ranks`: every rank is a multiple of 8; some block has rank 64 and some block rank 8.
All inputs are finite; a program needn't handle non-finite values.
Results may differ from the reference program's by a relative error of at most 0.0003.
Values may be sent and summed in bfloat16 or wider, within the bound.
No kernel may reach another device: no remote copies, remote signals or barrier semaphores. Data moves between devices by JAX's collectives and lax.ppermute only.
A program may use at most 128 MiB of HBM per device.

```python
import jax
import jax.numpy as jnp
from jax import lax

FFW = 3328
TOK_DEV = 512
BLOCK = 128
RANK_MAX = 64
D = 2048
TOKENS = 131072
BLOCKS = 16
N_GRP = 8
N_REP = 32


def draw_block_ranks(key, part):
    key = jax.random.fold_in(key, 7)
    key_levels, key_top, key_low = jax.random.split(key, 3)
    total_blocks = D // BLOCK
    levels = jax.random.randint(key_levels, (total_blocks,), 1, RANK_MAX // 8 + 1)
    highest = jax.random.randint(key_top, (), 0, total_blocks)
    lowest = (highest + 1 + jax.random.randint(key_low, (), 0, total_blocks - 1)) % total_blocks
    levels = levels.at[highest].set(RANK_MAX // 8).at[lowest].set(1)
    return (8 * levels).astype(jnp.int32)


def shard_levels(stream_key, dims, pieces, least, high):
    gain, own = 1.0, jax.random.fold_in(stream_key, 6)
    for position, parts in pieces:
        steps = jnp.exp(jax.random.uniform(jax.random.fold_in(own, position), (parts,), jnp.float32, least / len(pieces), high / len(pieces)))
        gain = gain * jnp.repeat(steps, dims[position] // parts).reshape([-1 if axis == position else 1 for axis in range(len(dims))])
    return gain


def noise(rng, dims, deviation, most, cuts=(), kind=jnp.bfloat16):
    values = deviation * jax.random.normal(rng, dims, jnp.float32)
    if cuts:
        values = values * shard_levels(rng, dims, cuts, -0.22, 0.18)
    return jnp.clip(values, -most, most).astype(kind)


def setup_inputs(seed: int = 0) -> dict:
    splits = jax.random.split(jax.random.key(seed), 6)
    hidden = noise(splits[0], (TOKENS, FFW), 1.0, 6.0, ((0, 256),))
    out_grad = noise(splits[1], (TOKENS, D), (TOK_DEV * N_GRP) ** -0.5, 0.09375, ((0, 256),))
    error_in = noise(splits[2], (N_REP, D, FFW), 1.0, 6.0, ((0, 32), (1, 8)))
    initial_basis = noise(splits[3], (BLOCKS, FFW, RANK_MAX), FFW ** -0.5, 0.109375, ((0, 8),))
    block_ranks = draw_block_ranks(jax.random.fold_in(splits[5], 71), 0)
    return dict(hidden=hidden, out_grad=out_grad, error_in=error_in, initial_basis=initial_basis, block_ranks=block_ranks)


def orthonormal_cols(projected, active):
    gram = jnp.einsum('bck,bcl->bkl', projected, projected, precision=lax.Precision.HIGHEST)
    paired = active[:, :, None] & active[:, None, :]
    gram = jnp.where(paired, gram, jnp.eye(gram.shape[-1], dtype=gram.dtype))
    lower = jnp.linalg.cholesky(gram)
    return lax.linalg.triangular_solve(lower, projected, left_side=False, lower=True, transpose_a=True)

def reference(hidden, out_grad, error_in, initial_basis, block_ranks):
    acts_all = hidden.reshape(N_GRP, N_REP, TOK_DEV, FFW)
    grads_all = out_grad.reshape(N_GRP, N_REP, TOK_DEV, D)

    def one_replica(replica):
        acts = lax.dynamic_index_in_dim(acts_all, replica, 1, keepdims=False).reshape(N_GRP * TOK_DEV, FFW)
        grads = lax.dynamic_index_in_dim(grads_all, replica, 1, keepdims=False).reshape(N_GRP * TOK_DEV, D)
        gradient = lax.dot_general(grads.astype(jnp.float32), acts.astype(jnp.float32), (((0,), (0,)), ((), ())), preferred_element_type=jnp.float32)
        return gradient + error_in[replica].astype(jnp.float32)
    combined = lax.map(one_replica, jnp.arange(N_REP, dtype=jnp.int32))
    blocks = combined.reshape(N_REP, BLOCKS, BLOCK, FFW)
    active = jnp.arange(RANK_MAX, dtype=jnp.int32)[None, :] < block_ranks[:, None]
    basis = initial_basis.astype(jnp.float32) * active[:, None, :].astype(jnp.float32)
    projected = jnp.einsum('rbcf,bfk->bck', blocks, basis, precision=lax.Precision.HIGHEST)
    ortho = orthonormal_cols(projected, active)
    next_basis = jnp.einsum('rbcf,bck->bfk', blocks, ortho, precision=lax.Precision.HIGHEST) / N_REP
    approx = jnp.einsum('bck,bfk->bcf', ortho, next_basis, precision=lax.Precision.HIGHEST)
    new_error = (blocks - approx[None]).reshape(N_REP, D, FFW)
    return (new_error, next_basis)
```

```python
import functools

import jax
import jax.numpy as jnp
from jax import lax
from jax.experimental import pallas as pl
from jax.experimental.pallas import tpu as pltpu
from jax.sharding import PartitionSpec as P

BLOCK = 128
RANK_MAX = 64
TILE = 256
PAD = 128
F32 = jnp.float32
BF16 = jnp.bfloat16
I16 = jnp.int16
PEAK = 32767.0
FINE = 64.0


def code_of(top):
    return jnp.ceil(jnp.log2(jnp.maximum(top, 1e-30)) * FINE) + 1.0


def size_of(code):
    return jnp.exp2(code * (1.0 / FINE))


def to_i16(x):
    return x.astype(jnp.int32).astype(I16)


def from_i16(x):
    return x.astype(jnp.int32).astype(F32)


def quantize(x):
    code = code_of(jnp.max(jnp.abs(x), axis=1, keepdims=True))
    return to_i16(jnp.round(x * (PEAK / size_of(code)))), code


def lanes(rows):
    return lax.broadcasted_iota(jnp.int32, (rows, PAD), 1)


def steps_of(codes):
    return size_of(from_i16(codes)) * (1.0 / PEAK)


def terms(x):
    hi = x.astype(BF16)
    rest = x - hi.astype(F32)
    return hi, rest.astype(BF16)


def dot(a, b, ca, cb):
    return lax.dot_general(a, b, (((ca,), (cb,)), ((), ())), preferred_element_type=F32)


def dot3(a, b, ca, cb):
    ah, al = terms(a)
    bh, bl = terms(b)
    return dot(ah, bh, ca, cb) + (dot(ah, bl, ca, cb) + dot(al, bh, ca, cb))


def grad_kernel(block, width, place, og, og_sib, h, h_sib, err, own, q1, q2, q3, lhs, codes):
    n = pl.program_id(0)
    tiles = width // TILE
    x, c = place[0] >> 1, place[0] & 1

    @pl.when(n == 0)
    def _():
        tok = og.shape[0]
        for d in range(4):
            owner = (x + d) & 3
            at = pl.multiple_of((owner * 2 + c) * 256 + block * BLOCK, BLOCK)
            lhs[d * BLOCK : (d + 1) * BLOCK, :tok] = og[:, pl.ds(at, BLOCK)].T
            at = pl.multiple_of(owner * 256 + block * BLOCK, BLOCK)
            lhs[d * BLOCK : (d + 1) * BLOCK, tok:] = og_sib[:, pl.ds(at, BLOCK)].T
        codes[...] = jnp.zeros_like(codes)

    tok = og.shape[0]
    total = dot(lhs[:, :tok], h[...], 1, 0) + dot(lhs[:, tok:], h_sib[...], 1, 0)
    own[...] = total[:BLOCK] + err[0].astype(F32)
    here = lanes(BLOCK) == n
    for d, out in ((1, q1), (2, q2), (3, q3)):
        part, code = quantize(total[d * BLOCK : (d + 1) * BLOCK])
        out[:, pl.ds(pl.multiple_of(n * TILE, TILE), TILE)] = part
        codes[d - 1] = jnp.where(here, code, codes[d - 1])

        @pl.when(n == tiles - 1)
        def _():
            out[:, width:] = to_i16(codes[d - 1])


def grad_chunk(place, og, og_sib, h, h_sib, err, block, first, width):
    tok, rows = og.shape
    full = lambda n, p: (0, 0)
    shape = jax.ShapeDtypeStruct((BLOCK, width + PAD), I16)
    return pl.pallas_call(
        functools.partial(grad_kernel, block, width),
        grid_spec=pltpu.PrefetchScalarGridSpec(
            num_scalar_prefetch=1,
            grid=(width // TILE,),
            in_specs=[
                pl.BlockSpec((tok, rows), full),
                pl.BlockSpec((tok, rows // 2), full),
                pl.BlockSpec((tok, TILE), lambda n, p: (0, n + first // TILE)),
                pl.BlockSpec((tok, TILE), lambda n, p: (0, n + first // TILE)),
                pl.BlockSpec((1, BLOCK, TILE), lambda n, p: (0, block, n + first // TILE)),
            ],
            out_specs=[pl.BlockSpec((BLOCK, TILE), lambda n, p: (0, n))]
            + [pl.BlockSpec((BLOCK, width + PAD), full)] * 3,
            scratch_shapes=[
                pltpu.VMEM((4 * BLOCK, 2 * tok), BF16),
                pltpu.VMEM((3, BLOCK, PAD), F32),
            ],
        ),
        out_shape=[jax.ShapeDtypeStruct((BLOCK, width), F32), shape, shape, shape],
        compiler_params=pltpu.CompilerParams(vmem_limit_bytes=30 << 20),
        cost_estimate=pl.CostEstimate(
            flops=2 * 4 * BLOCK * 2 * tok * width,
            bytes_accessed=tok * width * 4 + tok * rows * 3 + BLOCK * width * 12,
            transcendentals=0,
        ),
        name="chip_gradient",
    )(place, og, og_sib, h, h_sib, err)


def owner_kernel(width, own, r1, r2, r3, comb, zq):
    rows = own.shape[0]
    steps = [steps_of(r[:, width:]) for r in (r1, r2, r3)]
    codes = jnp.zeros((rows, PAD), F32)
    for n in range(width // TILE):
        cols = slice(n * TILE, (n + 1) * TILE)
        total = own[:, cols]
        for r, s in zip((r1, r2, r3), steps):
            total += from_i16(r[:, cols]) * s[:, n : n + 1]
        comb[:, cols] = total
        part, code = quantize(total)
        zq[:, cols] = part
        codes = jnp.where(lanes(rows) == n, code, codes)
    zq[:, width:] = to_i16(codes)


def owner_chunk(own, r1, r2, r3, width):
    rows = 32
    spec = pl.BlockSpec((rows, width + PAD), lambda n: (n, 0))
    flat = pl.BlockSpec((rows, width), lambda n: (n, 0))
    return pl.pallas_call(
        functools.partial(owner_kernel, width),
        grid=(BLOCK // rows,),
        in_specs=[flat, spec, spec, spec],
        out_specs=[flat, spec],
        out_shape=[
            jax.ShapeDtypeStruct((BLOCK, width), F32),
            jax.ShapeDtypeStruct((BLOCK, width + PAD), I16),
        ],
        compiler_params=pltpu.CompilerParams(vmem_limit_bytes=16 << 20),
        cost_estimate=pl.CostEstimate(
            flops=BLOCK * width * 30, bytes_accessed=BLOCK * width * 16, transcendentals=0
        ),
        name="sum_chips",
    )(own, r1, r2, r3)


def pair_sum(parts):
    while len(parts) > 1:
        half = len(parts) // 2
        parts = [parts[i] + parts[i + half] for i in range(half)]
    return parts[0]


def shard_kernel(width, count, *refs):
    ins, out = refs[:-1], refs[-1]
    if len(ins) == 1:
        ins = [ins[0].at[i] for i in range(count)]
    rows = out.shape[0]
    steps = [steps_of(r[:, width:]) for r in ins]
    codes = jnp.zeros((rows, PAD), F32)
    for n in range(width // TILE):
        cols = slice(n * TILE, (n + 1) * TILE)
        total = pair_sum([from_i16(r[:, cols]) * s[:, n : n + 1] for r, s in zip(ins, steps)])
        part, code = quantize(total)
        out[:, cols] = part
        codes = jnp.where(lanes(rows) == n, code, codes)
    out[:, width:] = to_i16(codes)


def shard_sum(width, count, *ins):
    rows = ins[0].shape[-2]
    return pl.pallas_call(
        functools.partial(shard_kernel, width, count),
        out_shape=jax.ShapeDtypeStruct((rows, width + PAD), I16),
        compiler_params=pltpu.CompilerParams(vmem_limit_bytes=16 << 20),
        cost_estimate=pl.CostEstimate(
            flops=count * rows * width * 10, bytes_accessed=count * rows * width * 2, transcendentals=0
        ),
        name="sum_replicas",
    )(*ins)


def factor_kernel(widths, replicas, *refs):
    count = len(widths)
    ranks, basis = refs[0], refs[1]
    sums, combs = refs[2 : 2 + count], refs[2 + count : 2 + 2 * count]
    new_error, next_t, mean = refs[2 + 2 * count :]
    rank = ranks[0]
    at = 0
    for s, width in zip(sums, widths):
        step = steps_of(s[:, width:])
        for n in range(width // TILE):
            cols = slice(n * TILE, (n + 1) * TILE)
            mean[:, at : at + TILE] = from_i16(s[:, cols]) * step[:, n : n + 1]
            at += TILE
    active = lax.broadcasted_iota(jnp.int32, (RANK_MAX, 1), 0) < rank
    active_row = lax.broadcasted_iota(jnp.int32, (1, RANK_MAX), 1) < rank
    hi, lo = terms(mean[...])
    base = basis[...]
    proj = dot(base, hi, 1, 1) + dot(base, lo, 1, 1)
    proj = jnp.where(active, proj, 0.0)
    gram = lax.dot_general(
        proj, proj, (((1,), (1,)), ((), ())), precision=lax.Precision.HIGHEST, preferred_element_type=F32
    )
    rows = lax.broadcasted_iota(jnp.int32, (RANK_MAX, RANK_MAX), 0)
    cols = lax.broadcasted_iota(jnp.int32, (RANK_MAX, RANK_MAX), 1)
    gram = jnp.where(active & active_row, gram, (rows == cols).astype(F32))
    index = lax.broadcasted_iota(jnp.int32, (RANK_MAX, 1), 0)
    ortho = proj
    for k in range(RANK_MAX):
        top = lax.rsqrt(gram[k : k + 1, k : k + 1])
        top_g = gram[k : k + 1, :] * top
        top_o = ortho[k : k + 1, :] * top
        below = jnp.where(index > k, gram[:, k : k + 1] * top, 0.0)
        gram = gram - below * top_g
        ortho = jnp.where(index == k, top_o, ortho - below * top_o)
    oh, ol = terms(ortho)
    back = (dot(oh, hi, 1, 0) + (dot(oh, lo, 1, 0) + dot(ol, hi, 1, 0))) * (1.0 / replicas)
    next_t[...] = back
    bh, bl = terms(back)
    at = 0
    for c, width in zip(combs, widths):
        part = slice(at, at + width)
        approx = dot(oh, bh[:, part], 0, 0) + (dot(oh, bl[:, part], 0, 0) + dot(ol, bh[:, part], 0, 0))
        new_error[:, part] = c[...] - approx
        at += width


def factor_block(rank, basis_t, sums, combs, widths, replicas):
    total = sum(widths)
    vmem = pl.BlockSpec(memory_space=pltpu.VMEM)
    return pl.pallas_call(
        functools.partial(factor_kernel, widths, replicas),
        in_specs=[pl.BlockSpec(memory_space=pltpu.SMEM)] + [vmem] * (1 + 2 * len(widths)),
        out_specs=[vmem, vmem],
        out_shape=[
            jax.ShapeDtypeStruct((BLOCK, total), F32),
            jax.ShapeDtypeStruct((RANK_MAX, total), F32),
        ],
        scratch_shapes=[pltpu.VMEM((BLOCK, total), F32)],
        compiler_params=pltpu.CompilerParams(vmem_limit_bytes=30 << 20),
        cost_estimate=pl.CostEstimate(
            flops=20 * BLOCK * total * RANK_MAX, bytes_accessed=BLOCK * total * 12, transcendentals=0
        ),
        name="factor",
    )(rank, basis_t, *sums, *combs)


def per_device(hidden, out_grad, error_in, initial_basis, block_ranks):
    replicas = 32
    deep, wide = 8, 4
    chips = 4
    tok, ffw = hidden.shape
    g = lax.axis_index("grp")
    core = g & 1
    place = jnp.reshape(g, (1,)).astype(jnp.int32)

    def core_perm():
        return [(x * 2 + c, x * 2 + 1 - c) for x in range(chips) for c in range(2)]

    def x_perm(d):
        return [(x * 2 + c, ((x + d) % chips) * 2 + c) for x in range(chips) for c in range(2)]

    def y_perm(d):
        return [(z * wide + y, z * wide + (y + d) % wide) for z in range(deep) for y in range(wide)]

    z_groups = [[z * wide + y for z in range(deep)] for y in range(wide)]

    split = out_grad.reshape(tok, chips, 2, 2 * BLOCK)
    away = lax.dynamic_index_in_dim(split, 1 - core, 2, keepdims=False).reshape(tok, -1)
    og_sib = lax.ppermute(away, "grp", core_perm())
    h_sib = lax.ppermute(hidden, "grp", core_perm())

    chunks = [(0, 0, ffw), (1, 0, 7 * TILE), (1, 7 * TILE, ffw - 7 * TILE)]
    basis_t = jnp.swapaxes(initial_basis, 1, 2)
    sums, combs, widths = [[], []], [[], []], [[], []]
    for block, first, width in chunks:
        own, *parts = grad_chunk(place, out_grad, og_sib, hidden, h_sib, error_in, block, first, width)
        got = [lax.ppermute(part, "grp", x_perm(d)) for d, part in zip((1, 2, 3), parts)]
        comb, zq = owner_chunk(own, *got, width)
        zq = lax.all_to_all(
            zq.reshape(deep, BLOCK // deep, width + PAD), "rep", 0, 0, tiled=True, axis_index_groups=z_groups
        )
        yq = shard_sum(width, deep, zq)
        others = [lax.ppermute(yq, "rep", y_perm(d)) for d in (1, 2, 3)]
        aq = shard_sum(width, wide, yq, *others)
        mq = lax.all_gather(aq, "rep", axis=0, tiled=True, axis_index_groups=z_groups)
        sums[block].append(mq)
        combs[block].append(comb)
        widths[block].append(width)

    errors, bases = [], []
    for block in range(2):
        e, q = factor_block(
            block_ranks[block : block + 1], basis_t[block], sums[block], combs[block], tuple(widths[block]), replicas
        )
        errors.append(e)
        bases.append(q)
    new_error = jnp.concatenate(errors, axis=0)[None]
    next_basis = jnp.swapaxes(jnp.stack(bases), 1, 2)
    return new_error, next_basis


def solution(mesh):
    return jax.shard_map(
        per_device,
        mesh=mesh,
        in_specs=(
            P(("grp", "rep"), None),
            P(("grp", "rep"), None),
            P("rep", "grp", None),
            P("grp", None, None),
            P("grp"),
        ),
        out_specs=(P("rep", "grp", None), P("grp", None, None)),
        check_vma=False,
    )
```

```python
import functools

import jax
import jax.numpy as jnp
from jax import lax
from jax.experimental import pallas as pl
from jax.experimental.pallas import tpu as pltpu
from jax.sharding import PartitionSpec as P

BLOCK = 128
RANK_MAX = 64
TILE = 256
LANE = 128
PAD = 128
F32 = jnp.float32
BF16 = jnp.bfloat16
I16 = jnp.int16
PEAK = 32767.0
SMALL = pl.CostEstimate(flops=1000, bytes_accessed=1000, transcendentals=0)
ANY = pl.BlockSpec(memory_space=pl.ANY)
VMEM = pl.BlockSpec(memory_space=pltpu.VMEM)
SMEM = pl.BlockSpec(memory_space=pltpu.SMEM)
FINE = 64.0


def code_of(top):
    return jnp.ceil(jnp.log2(jnp.maximum(top, 1e-30)) * FINE) + 1.0


def size_of(code):
    return jnp.exp2(code * (1.0 / FINE))


def to_i16(x):
    return x.astype(jnp.int32).astype(I16)


def from_i16(x):
    return x.astype(jnp.int32).astype(F32)


def quantize(x):
    code = code_of(jnp.max(jnp.abs(x), axis=0, keepdims=True))
    return to_i16(jnp.round(x * (PEAK / size_of(code)))), code


def steps_of(codes):
    return size_of(from_i16(codes)) * (1.0 / PEAK)


def terms(x):
    hi = x.astype(BF16)
    rest = x - hi.astype(F32)
    return hi, rest.astype(BF16)


def dot(a, b, ca, cb):
    return lax.dot_general(a, b, (((ca,), (cb,)), ((), ())), preferred_element_type=F32)


def dot3(a, b, ca, cb):
    ah, al = terms(a)
    bh, bl = terms(b)
    return dot(ah, bh, ca, cb) + (dot(ah, bl, ca, cb) + dot(al, bh, ca, cb))


def grad_kernel(block, width, place, og, og_sib, h, h_sib, err, *refs):
    out, lhs, codes = refs[-3:]
    half = pl.program_id(0)
    x, c = place[0] >> 1, place[0] & 1
    tok = og.shape[0]
    span = width // 2

    @pl.when(half == 0)
    def _():
        for owner in range(4):
            rows = slice(owner * BLOCK, (owner + 1) * BLOCK)
            at = pl.multiple_of(owner * 512 + c * 256 + block * BLOCK, BLOCK)
            lhs[rows, :tok] = og[:, pl.ds(at, BLOCK)].T
            at = owner * 256 + block * BLOCK
            lhs[rows, tok:] = og_sib[:, at : at + BLOCK].T
        codes[...] = jnp.zeros_like(codes)

    left, right = lhs[:, :tok], lhs[:, tok:]
    for at in range(0, span, TILE):
        size = min(TILE, span - at)
        cols = slice(at, at + size)
        total = dot(left, h[:, cols], 1, 0) + dot(right, h_sib[:, cols], 1, 0)
        memory = err[0, :, cols].astype(F32)
        for k in range(4):
            part = total[k * BLOCK : (k + 1) * BLOCK] + jnp.where(x == k, memory, 0.0)
            part, code = quantize(part)
            out[k, :, pl.ds(pl.multiple_of(half * span + at, LANE), size)] = part
            for i in range(size // LANE):
                t = half * (span // LANE) + at // LANE + i
                codes[k, pl.ds(t, 1)] = code[:, i * LANE : (i + 1) * LANE]

    @pl.when(half == 1)
    def _():
        for k in range(4):
            out[k, :, width:] = to_i16(codes[k])


def grad_chunk(place, og, og_sib, h, h_sib, err, block, after):
    tok, rows = og.shape
    width = h.shape[1]
    full = lambda n, p: (0, 0)
    return pl.pallas_call(
        functools.partial(grad_kernel, block, width),
        grid_spec=pltpu.PrefetchScalarGridSpec(
            num_scalar_prefetch=1,
            grid=(2,),
            in_specs=[
                pl.BlockSpec((tok, rows), full),
                pl.BlockSpec((tok, rows // 2), full),
                pl.BlockSpec((tok, width // 2), lambda n, p: (0, n)),
                pl.BlockSpec((tok, width // 2), lambda n, p: (0, n)),
                pl.BlockSpec((1, BLOCK, width // 2), lambda n, p: (0, block, n)),
            ]
            + [ANY] * len(after),
            out_specs=pl.BlockSpec((4, BLOCK, width + PAD), lambda n, p: (0, 0, 0)),
            scratch_shapes=[
                pltpu.VMEM((4 * BLOCK, 2 * tok), BF16),
                pltpu.VMEM((4, BLOCK, PAD), F32),
            ],
        ),
        out_shape=jax.ShapeDtypeStruct((4, BLOCK, width + PAD), I16),
        compiler_params=pltpu.CompilerParams(vmem_limit_bytes=60 << 20),
        cost_estimate=SMALL,
        name="chip_gradient",
    )(place, og, og_sib, h, h_sib, err, *after)


def pick_kernel(place, og, out):
    out[...] = og[...]


def pick(place, og):
    tok, rows = og.shape
    return pl.pallas_call(
        pick_kernel,
        grid_spec=pltpu.PrefetchScalarGridSpec(
            num_scalar_prefetch=1,
            grid=(4,),
            in_specs=[pl.BlockSpec((tok, 256), lambda n, p: (0, n * 2 + 1 - (p[0] & 1)))],
            out_specs=pl.BlockSpec((tok, 256), lambda n, p: (0, n)),
        ),
        out_shape=jax.ShapeDtypeStruct((tok, rows // 2), BF16),
        name="pick_columns",
    )(place, og)


QUARTER = BLOCK // 4


def pair_sum(parts):
    while len(parts) > 1:
        half = len(parts) // 2
        parts = [parts[i] + parts[i + half] for i in range(half)]
    return parts[0]


def owner_kernel(widths, place, *refs):
    ins, (comb, keep, s1, s2, s3, codes) = refs[:-6], refs[-6:]
    i = pl.program_id(0)
    width = sum(widths)
    at = 0
    for k, part in enumerate(widths):
        got, tail = ins[2 * k : 2 * k + 2]
        four = [got.at[j] for j in range(4)]
        steps = [steps_of(tail[j]) for j in range(4)]
        for n in range(part // LANE):
            cols = slice(n * LANE, (n + 1) * LANE)
            comb[:, at : at + LANE] = pair_sum(
                [from_i16(r[:, cols]) * s[n : n + 1] for r, s in zip(four, steps)]
            )
            at += LANE

    @pl.when(i == 3)
    def _():
        keep[...] = comb[...]

    for d, out in ((0, s1), (1, s2), (2, s3)):

        @pl.when(i == d)
        def _():
            codes[...] = jnp.zeros_like(codes)
            for n in range(width // LANE):
                cols = slice(n * LANE, (n + 1) * LANE)
                out[:, cols], codes[n : n + 1] = quantize(comb[:, cols])
            out[:, width:] = to_i16(codes[...])


def owner_chunk(y, pieces, widths, after):
    width = sum(widths)
    row = lambda n, p: ((n + 1 + p[0]) & 3, 0)
    full = lambda n, p: (0, 0)
    specs, ins = [], []
    for got, w in zip(pieces, widths):
        ins += [got, got]
        specs += [
            pl.BlockSpec((4, QUARTER, w), lambda n, p: (0, (n + 1 + p[0]) & 3, 0)),
            pl.BlockSpec((4, QUARTER, PAD), lambda n, p, w=w: (0, 0, w // PAD)),
        ]
    specs += [ANY] * len(after)
    shape = jax.ShapeDtypeStruct((QUARTER, width + PAD), I16)
    return pl.pallas_call(
        functools.partial(owner_kernel, widths),
        grid_spec=pltpu.PrefetchScalarGridSpec(
            num_scalar_prefetch=1,
            grid=(4,),
            in_specs=specs,
            out_specs=[pl.BlockSpec((QUARTER, width), row), pl.BlockSpec((QUARTER, width), full)]
            + [pl.BlockSpec((QUARTER, width + PAD), full)] * 3,
            scratch_shapes=[pltpu.VMEM((QUARTER, PAD), F32)],
        ),
        out_shape=[
            jax.ShapeDtypeStruct((BLOCK, width), F32),
            jax.ShapeDtypeStruct((QUARTER, width), F32),
            shape,
            shape,
            shape,
        ],
        compiler_params=pltpu.CompilerParams(vmem_limit_bytes=16 << 20),
        cost_estimate=SMALL,
        name="sum_chips",
    )(y, *ins, *after)


def shard_kernel(width, count, *refs):
    ins, (out, codes) = refs[:count], refs[-2:]
    steps = [None if r.dtype == F32 else steps_of(r[:, width:]) for r in ins]
    codes[...] = jnp.zeros_like(codes)
    for n in range(width // LANE):
        cols = slice(n * LANE, (n + 1) * LANE)
        total = pair_sum(
            [r[:, cols] if s is None else from_i16(r[:, cols]) * s[n : n + 1] for r, s in zip(ins, steps)]
        )
        out[:, cols], codes[n : n + 1] = quantize(total)
    out[:, width:] = to_i16(codes[...])


def shard_sum(width, ins, after):
    rows = ins[0].shape[0]
    return pl.pallas_call(
        functools.partial(shard_kernel, width, len(ins)),
        in_specs=[VMEM] * len(ins) + [ANY] * len(after),
        out_specs=VMEM,
        out_shape=jax.ShapeDtypeStruct((rows, width + PAD), I16),
        scratch_shapes=[pltpu.VMEM((rows, PAD), F32)],
        compiler_params=pltpu.CompilerParams(vmem_limit_bytes=16 << 20),
        cost_estimate=SMALL,
        name="sum_replicas",
    )(*ins, *after)


def cast_sums(sums, q, mean):
    width = mean.shape[1]
    for d, s in enumerate(sums):
        step = steps_of(s[:, width:])
        row = pl.multiple_of(((q + 4 - d) & 3) * QUARTER, QUARTER)
        for n in range(width // LANE):
            cols = slice(n * LANE, (n + 1) * LANE)
            mean[pl.ds(row, QUARTER), cols] = from_i16(s[:, cols]) * step[n : n + 1]


def factor_kernel(replicas, *refs):
    ranks, q, basis = refs[:3]
    sums, combs = (refs[3:7], refs[7:11]), refs[11:13]
    new_error, next_t, mean = refs[13:]
    row_at = lax.broadcasted_iota(jnp.int32, (8, 1), 0)
    tall = lax.broadcasted_iota(jnp.int32, (RANK_MAX, 1), 0)
    wide = lax.broadcasted_iota(jnp.int32, (1, RANK_MAX), 1)
    halves, grams, orthos, pivots = [], [], [], []
    for b in range(2):
        cast_sums(sums[b], q[0], mean)
        hi, lo = terms(mean[...])
        halves.append((hi, lo))
        rank = ranks[b]
        proj = dot(basis[b], hi, 1, 1) + dot(basis[b], lo, 1, 1)
        proj = jnp.where(tall < rank, proj, 0.0)
        gram = lax.dot_general(
            proj, proj, (((1,), (1,)), ((), ())), precision=lax.Precision.HIGHEST, preferred_element_type=F32
        )
        gram = jnp.where((tall < rank) & (wide < rank), gram, (tall == wide).astype(F32))
        grams.append([gram[8 * j : 8 * j + 8] for j in range(8)])
        orthos.append([proj[8 * j : 8 * j + 8] for j in range(8)])
        pivots.append([jnp.ones((8, 1), F32) for _ in range(8)])
    for k in range(RANK_MAX):
        at, own = divmod(k, 8)
        for gram, ortho, pivot in zip(grams, orthos, pivots):
            top = gram[at][own : own + 1, k : k + 1]
            pivot[at] = jnp.where(row_at == own, top, pivot[at])
            inverse = 1.0 / top
            top_g = gram[at][own : own + 1] * inverse
            top_o = ortho[at][own : own + 1] * inverse
            for j in range(at, 8):
                below = gram[j][:, k : k + 1]
                if j == at:
                    below = jnp.where(row_at > own, below, 0.0)
                gram[j] = gram[j] - below * top_g
                ortho[j] = ortho[j] - below * top_o
    for b in range(2):
        hi, lo = halves[b]
        scaled = [o * lax.rsqrt(p) for o, p in zip(orthos[b], pivots[b])]
        oh, ol = terms(jnp.concatenate(scaled, axis=0))
        back = (dot(oh, hi, 1, 0) + (dot(oh, lo, 1, 0) + dot(ol, hi, 1, 0))) * (1.0 / replicas)
        next_t[b] = back
        bh, bl = terms(back)
        approx = dot(oh, bh, 0, 0) + (dot(oh, bl, 0, 0) + dot(ol, bh, 0, 0))
        new_error[0, b * BLOCK : (b + 1) * BLOCK] = combs[b][...] - approx


def factor_blocks(ranks, q, basis_t, sums, combs, replicas):
    blocks, _, total = basis_t.shape
    return pl.pallas_call(
        functools.partial(factor_kernel, replicas),
        in_specs=[SMEM, SMEM] + [VMEM] * 11,
        out_specs=[VMEM, VMEM],
        out_shape=[
            jax.ShapeDtypeStruct((1, blocks * BLOCK, total), F32),
            jax.ShapeDtypeStruct((blocks, RANK_MAX, total), F32),
        ],
        scratch_shapes=[pltpu.VMEM((BLOCK, total), F32)],
        compiler_params=pltpu.CompilerParams(vmem_limit_bytes=40 << 20),
        cost_estimate=SMALL,
        name="factor",
    )(ranks, q, basis_t, *sums[0], *sums[1], *combs)


def per_device(hidden, out_grad, error_in, initial_basis, block_ranks):
    deep, wide = 8, 4
    replicas = deep * wide
    chips = 4
    g, r = lax.axis_index("grp"), lax.axis_index("rep")
    place = jnp.reshape(g, (1,)).astype(jnp.int32)
    q = jnp.reshape(jnp.where((g & 1) == 0, r & 3, r >> 3), (1,)).astype(jnp.int32)

    core_perm = [(x * 2 + c, x * 2 + 1 - c) for x in range(chips) for c in range(2)]
    x_groups = [[x * 2 + c for x in range(chips)] for c in range(2)]

    def move(array, to):
        pairs = []
        for k in range(2 * chips):
            for z in range(deep):
                for i in range(wide):
                    z2, i2 = to(k & 1, z, i)
                    pairs.append((k * replicas + z * wide + i, k * replicas + (z2 % deep) * wide + i2 % wide))
        return lax.ppermute(array, ("grp", "rep"), pairs)

    def first(d):
        return lambda c, z, i: (z + 2 * d, i) if c else (z, i + d)

    def second(d):
        return lambda c, z, i: (z, i + d) if c else (z + 2 * d, i)

    og_sib = lax.ppermute(pick(place, out_grad), "grp", core_perm)
    h_sib = lax.ppermute(hidden, "grp", core_perm)

    pieces, last = [], []
    for block in range(2):
        last.append(grad_chunk(place, out_grad, og_sib, hidden, h_sib, error_in, block, last))
        pieces.append([lax.all_to_all(last[-1], "grp", 0, 0, tiled=True, axis_index_groups=x_groups)])

    def reduce_rows(block, after):
        comb, keep, *sends = owner_chunk(q, pieces[block], (hidden.shape[1],), after)
        return comb, keep, [move(s, first(d)) for d, s in zip((1, 2, 3), sends)]

    def exchange(part):
        return [part] + [move(part, second(d)) for d in (1, 2, 3)]

    def pair(part):
        return [part, move(part, lambda c, z, i: (z ^ 1, i))]

    def gather(part):
        return [part] + [move(part, first(d)) for d in (1, 2, 3)]

    width = hidden.shape[1]
    basis_t = jnp.swapaxes(initial_basis, 1, 2)

    comb_a, keep, got = reduce_rows(0, last[-1:])
    a1 = shard_sum(width, [keep, *got], [])
    a2 = shard_sum(width, exchange(a1), [])
    comb_b, keep, got = reduce_rows(1, [a2])
    a3 = shard_sum(width, pair(a2), [keep])
    b1 = shard_sum(width, [keep, *got], [a3])
    b2 = shard_sum(width, exchange(b1), [])
    b3 = shard_sum(width, pair(b2), [])
    new_error, next_t = factor_blocks(
        block_ranks, q, basis_t, (gather(a3), gather(b3)), (comb_a, comb_b), replicas
    )
    return new_error, jnp.swapaxes(next_t, 1, 2)


def solution(mesh):
    return jax.shard_map(
        per_device,
        mesh=mesh,
        in_specs=(
            P(("grp", "rep"), None),
            P(("grp", "rep"), None),
            P("rep", "grp", None),
            P("grp", None, None),
            P("grp"),
        ),
        out_specs=(P("rep", "grp", None), P("grp", None, None)),
        check_vma=False,
    )
```

```python
import functools

import jax
import jax.numpy as jnp
from jax import lax
from jax.experimental import pallas as pl
from jax.experimental.pallas import tpu as pltpu
from jax.sharding import PartitionSpec as P

BLOCK = 128
RANK_MAX = 64
TILE = 256
LANE = 128
PAD = 128
F32 = jnp.float32
BF16 = jnp.bfloat16
I16 = jnp.int16
PEAK = 32767.0
SMALL = pl.CostEstimate(flops=1000, bytes_accessed=1000, transcendentals=0)
ANY = pl.BlockSpec(memory_space=pl.ANY)
VMEM = pl.BlockSpec(memory_space=pltpu.VMEM)
SMEM = pl.BlockSpec(memory_space=pltpu.SMEM)
FINE = 64.0


def code_of(top):
    return jnp.ceil(jnp.log2(jnp.maximum(top, 1e-30)) * FINE) + 1.0


def size_of(code):
    return jnp.exp2(code * (1.0 / FINE))


def to_i16(x):
    return x.astype(jnp.int32).astype(I16)


def from_i16(x):
    return x.astype(jnp.int32).astype(F32)


def quantize(x):
    code = code_of(jnp.max(jnp.abs(x), axis=0, keepdims=True))
    return to_i16(jnp.round(x * (PEAK / size_of(code)))), code


def steps_of(codes):
    return size_of(from_i16(codes)) * (1.0 / PEAK)


def terms(x):
    hi = x.astype(BF16)
    rest = x - hi.astype(F32)
    return hi, rest.astype(BF16)


def dot(a, b, ca, cb):
    return lax.dot_general(a, b, (((ca,), (cb,)), ((), ())), preferred_element_type=F32)


def dot3(a, b, ca, cb):
    ah, al = terms(a)
    bh, bl = terms(b)
    return dot(ah, bh, ca, cb) + (dot(ah, bl, ca, cb) + dot(al, bh, ca, cb))


def grad_kernel(block, place, og, og_sib, h, h_sib, err, *refs):
    up, down, keep, lhs, codes = refs[-5:]
    half = pl.program_id(0)
    x, c = place[0] >> 1, place[0] & 1
    tok, span = h.shape

    @pl.when(half == 0)
    def _():
        for k in range(4):
            rows = slice(k * BLOCK, (k + 1) * BLOCK)
            owner = (x + k) & 3
            at = pl.multiple_of(owner * 512 + c * 256 + block * BLOCK, BLOCK)
            lhs[rows, :tok] = og[:, pl.ds(at, BLOCK)].T
            at = pl.multiple_of(owner * 256 + block * BLOCK, BLOCK)
            lhs[rows, tok:] = og_sib[:, pl.ds(at, BLOCK)].T
        codes[...] = jnp.zeros_like(codes)

    def work(slots):
        left, right = lhs[:, :tok], lhs[:, tok:]
        for at in range(0, span, TILE):
            size = min(TILE, span - at)
            cols = slice(at, at + size)
            total = dot(left, h[:, cols], 1, 0) + dot(right, h_sib[:, cols], 1, 0)
            for k, (out, slot) in enumerate(slots):
                part = total[k * BLOCK : (k + 1) * BLOCK]
                if k == 0:
                    part += err[0, :, cols].astype(F32)
                out[slot, :, cols], code = quantize(part)
                for i in range(size // LANE):
                    codes[k, at // LANE + i : at // LANE + i + 1] = code[:, i * LANE : (i + 1) * LANE]
        for k, (out, slot) in enumerate(slots):
            out[slot, :, span:] = to_i16(codes[k])

    @pl.when(half == 0)
    def _():
        work(((keep, 2), (keep, 0), (up, 0), (down, 1)))

    @pl.when(half == 1)
    def _():
        work(((keep, 3), (up, 1), (down, 0), (keep, 1)))


def grad_chunk(place, og, og_sib, h, h_sib, err, block, after):
    tok, rows = og.shape
    span = h.shape[1] // 2
    full = lambda n, p: (0, 0)
    fixed = lambda n, p: (0, 0, 0)
    return pl.pallas_call(
        functools.partial(grad_kernel, block),
        grid_spec=pltpu.PrefetchScalarGridSpec(
            num_scalar_prefetch=1,
            grid=(2,),
            in_specs=[
                pl.BlockSpec((tok, rows), full),
                pl.BlockSpec((tok, rows // 2), full),
                pl.BlockSpec((tok, span), lambda n, p: (0, n)),
                pl.BlockSpec((tok, span), lambda n, p: (0, n)),
                pl.BlockSpec((1, BLOCK, span), lambda n, p: (0, block, n)),
            ]
            + [ANY] * len(after),
            out_specs=[pl.BlockSpec((n, BLOCK, span + PAD), fixed) for n in (2, 2, 4)],
            scratch_shapes=[
                pltpu.VMEM((4 * BLOCK, 2 * tok), BF16),
                pltpu.VMEM((4, BLOCK, PAD), F32),
            ],
        ),
        out_shape=[jax.ShapeDtypeStruct((n, BLOCK, span + PAD), I16) for n in (2, 2, 4)],
        compiler_params=pltpu.CompilerParams(vmem_limit_bytes=60 << 20),
        cost_estimate=SMALL,
        name="chip_gradient",
    )(place, og, og_sib, h, h_sib, err, *after)


def relay_kernel(keep, got_up, got_down, *refs):
    up, down, codes = refs[-3:]
    span = up.shape[2] - PAD
    codes[...] = jnp.zeros_like(codes)
    for slot, got, out in ((0, got_up, up), (1, got_down, down)):
        mine, others = steps_of(keep[slot, :QUARTER, span:]), steps_of(got[0, :QUARTER, span:])
        for n in range(span // LANE):
            cols = slice(n * LANE, (n + 1) * LANE)
            total = from_i16(keep[slot, :, cols]) * mine[n : n + 1] + from_i16(got[0, :, cols]) * others[n : n + 1]
            out[0, :, cols], codes[n : n + 1] = quantize(total)
        out[0, :, span:] = to_i16(codes[...])


def relay(keep, got_up, got_down, after):
    wide = keep.shape[2]
    fixed = lambda n: (0, 0, 0)
    one = pl.BlockSpec((1, BLOCK, wide), fixed)
    return pl.pallas_call(
        relay_kernel,
        grid=(1,),
        in_specs=[pl.BlockSpec((2, BLOCK, wide), fixed), one, one] + [ANY] * len(after),
        out_specs=[one, one],
        out_shape=[jax.ShapeDtypeStruct((1, BLOCK, wide), I16)] * 2,
        scratch_shapes=[pltpu.VMEM((BLOCK, PAD), F32)],
        compiler_params=pltpu.CompilerParams(vmem_limit_bytes=16 << 20),
        cost_estimate=SMALL,
        name="add_on_the_way",
    )(keep, got_up, got_down, *after)


def pick_kernel(place, og, out):
    out[...] = og[...]


def pick(place, og):
    tok, rows = og.shape
    return pl.pallas_call(
        pick_kernel,
        grid_spec=pltpu.PrefetchScalarGridSpec(
            num_scalar_prefetch=1,
            grid=(4,),
            in_specs=[pl.BlockSpec((tok, 256), lambda n, p: (0, n * 2 + 1 - (p[0] & 1)))],
            out_specs=pl.BlockSpec((tok, 256), lambda n, p: (0, n)),
        ),
        out_shape=jax.ShapeDtypeStruct((tok, rows // 2), BF16),
        name="pick_columns",
    )(place, og)


QUARTER = BLOCK // 4


def pair_sum(parts):
    while len(parts) > 1:
        half = len(parts) // 2
        parts = [parts[i] + parts[i + half] for i in range(half)]
    return parts[0]


def owner_kernel(place, *refs):
    (comb, keep, s1, s2, s3, codes) = refs[-6:]
    own, own_c, up, up_c, down, down_c, sum_up, sum_up_c, sum_down, sum_down_c = refs[:10]
    i = pl.program_id(0)
    width = comb.shape[1]
    span = width // 2
    for half, three in (
        (0, ((own, own_c, 2), (down, down_c, 1), (sum_up, sum_up_c, 0))),
        (1, ((own, own_c, 3), (up, up_c, 1), (sum_down, sum_down_c, 0))),
    ):
        steps = [steps_of(tail[slot]) for _, tail, slot in three]
        for n in range(span // LANE):
            cols = slice(n * LANE, (n + 1) * LANE)
            a, b, c = [from_i16(r[slot, :, cols]) * s[n : n + 1] for (r, _, slot), s in zip(three, steps)]
            comb[:, half * span + n * LANE : half * span + (n + 1) * LANE] = a + b + c

    @pl.when(i == 3)
    def _():
        keep[...] = comb[...]

    for d, out in ((0, s1), (1, s2), (2, s3)):

        @pl.when(i == d)
        def _():
            codes[...] = jnp.zeros_like(codes)
            for n in range(width // LANE):
                cols = slice(n * LANE, (n + 1) * LANE)
                out[:, cols], codes[n : n + 1] = quantize(comb[:, cols])
            out[:, width:] = to_i16(codes[...])


def owner_chunk(y, pieces, after):
    span = pieces[0].shape[2] - PAD
    width = 2 * span
    row = lambda n, p: ((n + 1 + p[0]) & 3, 0)
    full = lambda n, p: (0, 0)
    specs, ins = [], []
    for got in pieces:
        ins += [got, got]
        specs += [
            pl.BlockSpec((got.shape[0], QUARTER, span), lambda n, p: (0, (n + 1 + p[0]) & 3, 0)),
            pl.BlockSpec((got.shape[0], QUARTER, PAD), lambda n, p: (0, 0, span // PAD)),
        ]
    specs += [ANY] * len(after)
    shape = jax.ShapeDtypeStruct((QUARTER, width + PAD), I16)
    return pl.pallas_call(
        owner_kernel,
        grid_spec=pltpu.PrefetchScalarGridSpec(
            num_scalar_prefetch=1,
            grid=(4,),
            in_specs=specs,
            out_specs=[pl.BlockSpec((QUARTER, width), row), pl.BlockSpec((QUARTER, width), full)]
            + [pl.BlockSpec((QUARTER, width + PAD), full)] * 3,
            scratch_shapes=[pltpu.VMEM((QUARTER, PAD), F32)],
        ),
        out_shape=[
            jax.ShapeDtypeStruct((BLOCK, width), F32),
            jax.ShapeDtypeStruct((QUARTER, width), F32),
            shape,
            shape,
            shape,
        ],
        compiler_params=pltpu.CompilerParams(vmem_limit_bytes=16 << 20),
        cost_estimate=SMALL,
        name="sum_chips",
    )(y, *ins, *after)


def shard_kernel(width, count, *refs):
    ins, (out, codes) = refs[:count], refs[-2:]
    steps = [None if r.dtype == F32 else steps_of(r[:, width:]) for r in ins]
    codes[...] = jnp.zeros_like(codes)
    for n in range(width // LANE):
        cols = slice(n * LANE, (n + 1) * LANE)
        total = pair_sum(
            [r[:, cols] if s is None else from_i16(r[:, cols]) * s[n : n + 1] for r, s in zip(ins, steps)]
        )
        out[:, cols], codes[n : n + 1] = quantize(total)
    out[:, width:] = to_i16(codes[...])


def shard_sum(width, ins, after):
    rows = ins[0].shape[0]
    return pl.pallas_call(
        functools.partial(shard_kernel, width, len(ins)),
        in_specs=[VMEM] * len(ins) + [ANY] * len(after),
        out_specs=VMEM,
        out_shape=jax.ShapeDtypeStruct((rows, width + PAD), I16),
        scratch_shapes=[pltpu.VMEM((rows, PAD), F32)],
        compiler_params=pltpu.CompilerParams(vmem_limit_bytes=16 << 20),
        cost_estimate=SMALL,
        name="sum_replicas",
    )(*ins, *after)


def cast_sums(sums, q, mean):
    width = mean.shape[1]
    for d, s in enumerate(sums):
        step = steps_of(s[:, width:])
        row = pl.multiple_of(((q + 4 - d) & 3) * QUARTER, QUARTER)
        for n in range(width // LANE):
            cols = slice(n * LANE, (n + 1) * LANE)
            mean[pl.ds(row, QUARTER), cols] = from_i16(s[:, cols]) * step[n : n + 1]


def factor_kernel(replicas, *refs):
    ranks, q, basis = refs[:3]
    sums, combs = (refs[3:7], refs[7:11]), refs[11:13]
    new_error, next_t, mean = refs[13:]
    row_at = lax.broadcasted_iota(jnp.int32, (8, 1), 0)
    tall = lax.broadcasted_iota(jnp.int32, (RANK_MAX, 1), 0)
    wide = lax.broadcasted_iota(jnp.int32, (1, RANK_MAX), 1)
    halves, grams, orthos, pivots = [], [], [], []
    for b in range(2):
        cast_sums(sums[b], q[0], mean)
        hi, lo = terms(mean[...])
        halves.append((hi, lo))
        rank = ranks[b]
        proj = dot(basis[b], hi, 1, 1) + dot(basis[b], lo, 1, 1)
        proj = jnp.where(tall < rank, proj, 0.0)
        gram = lax.dot_general(
            proj, proj, (((1,), (1,)), ((), ())), precision=lax.Precision.HIGHEST, preferred_element_type=F32
        )
        gram = jnp.where((tall < rank) & (wide < rank), gram, (tall == wide).astype(F32))
        grams.append([gram[8 * j : 8 * j + 8] for j in range(8)])
        orthos.append([proj[8 * j : 8 * j + 8] for j in range(8)])
        pivots.append([jnp.ones((8, 1), F32) for _ in range(8)])
    for k in range(RANK_MAX):
        at, own = divmod(k, 8)
        for gram, ortho, pivot in zip(grams, orthos, pivots):
            top = gram[at][own : own + 1, k : k + 1]
            pivot[at] = jnp.where(row_at == own, top, pivot[at])
            inverse = 1.0 / top
            top_g = gram[at][own : own + 1] * inverse
            top_o = ortho[at][own : own + 1] * inverse
            for j in range(at, 8):
                below = gram[j][:, k : k + 1]
                if j == at:
                    below = jnp.where(row_at > own, below, 0.0)
                gram[j] = gram[j] - below * top_g
                ortho[j] = ortho[j] - below * top_o
    for b in range(2):
        hi, lo = halves[b]
        scaled = [o * lax.rsqrt(p) for o, p in zip(orthos[b], pivots[b])]
        oh, ol = terms(jnp.concatenate(scaled, axis=0))
        back = (dot(oh, hi, 1, 0) + (dot(oh, lo, 1, 0) + dot(ol, hi, 1, 0))) * (1.0 / replicas)
        next_t[b] = back
        bh, bl = terms(back)
        approx = dot(oh, bh, 0, 0) + (dot(oh, bl, 0, 0) + dot(ol, bh, 0, 0))
        new_error[0, b * BLOCK : (b + 1) * BLOCK] = combs[b][...] - approx


def factor_blocks(ranks, q, basis_t, sums, combs, replicas):
    blocks, _, total = basis_t.shape
    return pl.pallas_call(
        functools.partial(factor_kernel, replicas),
        in_specs=[SMEM, SMEM] + [VMEM] * 11,
        out_specs=[VMEM, VMEM],
        out_shape=[
            jax.ShapeDtypeStruct((1, blocks * BLOCK, total), F32),
            jax.ShapeDtypeStruct((blocks, RANK_MAX, total), F32),
        ],
        scratch_shapes=[pltpu.VMEM((BLOCK, total), F32)],
        compiler_params=pltpu.CompilerParams(vmem_limit_bytes=40 << 20),
        cost_estimate=SMALL,
        name="factor",
    )(ranks, q, basis_t, *sums[0], *sums[1], *combs)


def per_device(hidden, out_grad, error_in, initial_basis, block_ranks):
    deep, wide = 8, 4
    replicas = deep * wide
    chips = 4
    g, r = lax.axis_index("grp"), lax.axis_index("rep")
    place = jnp.reshape(g, (1,)).astype(jnp.int32)
    q = jnp.reshape(jnp.where((g & 1) == 0, r & 3, r >> 3), (1,)).astype(jnp.int32)

    core_perm = [(x * 2 + c, x * 2 + 1 - c) for x in range(chips) for c in range(2)]

    def move(array, to):
        pairs = []
        for k in range(2 * chips):
            for z in range(deep):
                for i in range(wide):
                    z2, i2 = to(k & 1, z, i)
                    pairs.append((k * replicas + z * wide + i, k * replicas + (z2 % deep) * wide + i2 % wide))
        return lax.ppermute(array, ("grp", "rep"), pairs)

    def first(d):
        return lambda c, z, i: (z + 2 * d, i) if c else (z, i + d)

    def second(d):
        return lambda c, z, i: (z, i + d) if c else (z + 2 * d, i)

    og_sib = lax.ppermute(pick(place, out_grad), "grp", core_perm)
    h_sib = lax.ppermute(hidden, "grp", core_perm)

    def along_x(array, d):
        pairs = [(x * 2 + c, ((x + d) % chips) * 2 + c) for x in range(chips) for c in range(2)]
        return lax.ppermute(array, "grp", pairs)

    def start_x(block, after):
        up, down, keep = grad_chunk(place, out_grad, og_sib, hidden, h_sib, error_in, block, after)
        return keep, along_x(up, 1), along_x(down, -1)

    def add_x(pieces, after):
        up, down = relay(*pieces, after)
        return [*pieces, along_x(up, 1), along_x(down, -1)]

    def reduce_rows(pieces, after):
        comb, keep, *sends = owner_chunk(q, pieces, after)
        return comb, keep, [move(s, first(d)) for d, s in zip((1, 2, 3), sends)]

    def exchange(part):
        return [part] + [move(part, second(d)) for d in (1, 2, 3)]

    def pair(part):
        return [part, move(part, lambda c, z, i: (z ^ 1, i))]

    def gather(part):
        return [part] + [move(part, first(d)) for d in (1, 2, 3)]

    width = hidden.shape[1]
    basis_t = jnp.swapaxes(initial_basis, 1, 2)

    a = start_x(0, [])
    b = start_x(1, [a[0]])
    a = add_x(a, [b[0]])
    comb_a, keep_a, got_a = reduce_rows(a, [])
    b = add_x(b, [keep_a])
    comb_b, keep_b, got_b = reduce_rows(b, [])
    a1 = shard_sum(width, [keep_a, *got_a], [keep_b])
    b1 = shard_sum(width, [keep_b, *got_b], [a1])
    a2 = shard_sum(width, exchange(a1), [b1])
    b2 = shard_sum(width, exchange(b1), [a2])
    a3 = shard_sum(width, pair(a2), [b2])
    b3 = shard_sum(width, pair(b2), [a3])
    new_error, next_t = factor_blocks(
        block_ranks, q, basis_t, (gather(a3), gather(b3)), (comb_a, comb_b), replicas
    )
    return new_error, jnp.swapaxes(next_t, 1, 2)


def solution(mesh):
    return jax.shard_map(
        per_device,
        mesh=mesh,
        in_specs=(
            P(("grp", "rep"), None),
            P(("grp", "rep"), None),
            P("rep", "grp", None),
            P("grp", None, None),
            P("grp"),
        ),
        out_specs=(P("rep", "grp", None), P("grp", None, None)),
        check_vma=False,
    )
```

```python
import functools

import jax
import jax.numpy as jnp
from jax import lax
from jax.experimental import pallas as pl
from jax.experimental.pallas import tpu as pltpu
from jax.sharding import PartitionSpec as P

BLOCK = 128
RANK_MAX = 64
TILE = 256
LANE = 128
PAD = 128
F32 = jnp.float32
BF16 = jnp.bfloat16
I16 = jnp.int16
PEAK = 32767.0
SMALL = pl.CostEstimate(flops=1000, bytes_accessed=1000, transcendentals=0)
ANY = pl.BlockSpec(memory_space=pl.ANY)
VMEM = pl.BlockSpec(memory_space=pltpu.VMEM)
SMEM = pl.BlockSpec(memory_space=pltpu.SMEM)
FINE = 64.0


def code_of(top):
    return jnp.ceil(jnp.log2(jnp.maximum(top, 1e-30)) * FINE) + 1.0


def size_of(code):
    return jnp.exp2(code * (1.0 / FINE))


def to_i16(x):
    return x.astype(jnp.int32).astype(I16)


def from_i16(x):
    return x.astype(jnp.int32).astype(F32)


def quantize(x):
    code = code_of(jnp.max(jnp.abs(x), axis=0, keepdims=True))
    return to_i16(jnp.round(x * (PEAK / size_of(code)))), code


def steps_of(codes):
    return size_of(from_i16(codes)) * (1.0 / PEAK)


def terms(x):
    hi = x.astype(BF16)
    rest = x - hi.astype(F32)
    return hi, rest.astype(BF16)


def dot(a, b, ca, cb):
    return lax.dot_general(a, b, (((ca,), (cb,)), ((), ())), preferred_element_type=F32)


def dot3(a, b, ca, cb):
    ah, al = terms(a)
    bh, bl = terms(b)
    return dot(ah, bh, ca, cb) + (dot(ah, bl, ca, cb) + dot(al, bh, ca, cb))


def grad_kernel(block, place, og, og_sib, h, h_sib, err, *refs):
    up, down, keep, lhs, codes = refs[-5:]
    half = pl.program_id(0)
    x, c = place[0] >> 1, place[0] & 1
    tok, span = h.shape

    @pl.when(half == 0)
    def _():
        for k in range(4):
            rows = slice(k * BLOCK, (k + 1) * BLOCK)
            owner = (x + k) & 3
            at = pl.multiple_of(owner * 512 + c * 256 + block * BLOCK, BLOCK)
            lhs[rows, :tok] = og[:, pl.ds(at, BLOCK)].T
            at = pl.multiple_of(owner * 256 + block * BLOCK, BLOCK)
            lhs[rows, tok:] = og_sib[:, pl.ds(at, BLOCK)].T
        codes[...] = jnp.zeros_like(codes)

    def work(slots):
        left, right = lhs[:, :tok], lhs[:, tok:]
        for at in range(0, span, TILE):
            size = min(TILE, span - at)
            cols = slice(at, at + size)
            total = dot(left, h[:, cols], 1, 0) + dot(right, h_sib[:, cols], 1, 0)
            for k, (out, slot) in enumerate(slots):
                part = total[k * BLOCK : (k + 1) * BLOCK]
                if k == 0:
                    part += err[0, :, cols].astype(F32)
                out[slot, :, cols], code = quantize(part)
                for i in range(size // LANE):
                    codes[k, at // LANE + i : at // LANE + i + 1] = code[:, i * LANE : (i + 1) * LANE]
        for k, (out, slot) in enumerate(slots):
            out[slot, :, span:] = to_i16(codes[k])

    @pl.when(half == 0)
    def _():
        work(((keep, 2), (keep, 0), (up, 0), (down, 1)))

    @pl.when(half == 1)
    def _():
        work(((keep, 3), (up, 1), (down, 0), (keep, 1)))


def grad_chunk(place, og, og_sib, h, h_sib, err, block, after):
    tok, rows = og.shape
    span = h.shape[1] // 2
    full = lambda n, p: (0, 0)
    fixed = lambda n, p: (0, 0, 0)
    return pl.pallas_call(
        functools.partial(grad_kernel, block),
        grid_spec=pltpu.PrefetchScalarGridSpec(
            num_scalar_prefetch=1,
            grid=(2,),
            in_specs=[
                pl.BlockSpec((tok, rows), full),
                pl.BlockSpec((tok, rows // 2), full),
                pl.BlockSpec((tok, span), lambda n, p: (0, n)),
                pl.BlockSpec((tok, span), lambda n, p: (0, n)),
                pl.BlockSpec((1, BLOCK, span), lambda n, p: (0, block, n)),
            ]
            + [ANY] * len(after),
            out_specs=[pl.BlockSpec((n, BLOCK, span + PAD), fixed) for n in (2, 2, 4)],
            scratch_shapes=[
                pltpu.VMEM((4 * BLOCK, 2 * tok), BF16),
                pltpu.VMEM((4, BLOCK, PAD), F32),
            ],
        ),
        out_shape=[jax.ShapeDtypeStruct((n, BLOCK, span + PAD), I16) for n in (2, 2, 4)],
        compiler_params=pltpu.CompilerParams(vmem_limit_bytes=60 << 20),
        cost_estimate=SMALL,
        name="chip_gradient",
    )(place, og, og_sib, h, h_sib, err, *after)


def relay_kernel(keep, got_up, got_down, *refs):
    up, down, codes = refs[-3:]
    span = up.shape[2] - PAD
    codes[...] = jnp.zeros_like(codes)
    for slot, got, out in ((0, got_up, up), (1, got_down, down)):
        mine, others = steps_of(keep[slot, :QUARTER, span:]), steps_of(got[0, :QUARTER, span:])
        for n in range(span // LANE):
            cols = slice(n * LANE, (n + 1) * LANE)
            total = from_i16(keep[slot, :, cols]) * mine[n : n + 1] + from_i16(got[0, :, cols]) * others[n : n + 1]
            out[0, :, cols], codes[n : n + 1] = quantize(total)
        out[0, :, span:] = to_i16(codes[...])


def relay(keep, got_up, got_down, after):
    wide = keep.shape[2]
    fixed = lambda n: (0, 0, 0)
    one = pl.BlockSpec((1, BLOCK, wide), fixed)
    return pl.pallas_call(
        relay_kernel,
        grid=(1,),
        in_specs=[pl.BlockSpec((2, BLOCK, wide), fixed), one, one] + [ANY] * len(after),
        out_specs=[one, one],
        out_shape=[jax.ShapeDtypeStruct((1, BLOCK, wide), I16)] * 2,
        scratch_shapes=[pltpu.VMEM((BLOCK, PAD), F32)],
        compiler_params=pltpu.CompilerParams(vmem_limit_bytes=16 << 20),
        cost_estimate=SMALL,
        name="add_on_the_way",
    )(keep, got_up, got_down, *after)


def pick_kernel(place, og, out):
    out[...] = og[...]


def pick(place, og):
    tok, rows = og.shape
    return pl.pallas_call(
        pick_kernel,
        grid_spec=pltpu.PrefetchScalarGridSpec(
            num_scalar_prefetch=1,
            grid=(4,),
            in_specs=[pl.BlockSpec((tok, 256), lambda n, p: (0, n * 2 + 1 - (p[0] & 1)))],
            out_specs=pl.BlockSpec((tok, 256), lambda n, p: (0, n)),
        ),
        out_shape=jax.ShapeDtypeStruct((tok, rows // 2), BF16),
        name="pick_columns",
    )(place, og)


QUARTER = BLOCK // 4


def pair_sum(parts):
    while len(parts) > 1:
        half = len(parts) // 2
        parts = [parts[i] + parts[i + half] for i in range(half)]
    return parts[0]


def owner_kernel(place, *refs):
    (comb, keep, s1, s2, s3, codes) = refs[-6:]
    own, own_c, up, up_c, down, down_c, sum_up, sum_up_c, sum_down, sum_down_c = refs[:10]
    i = pl.program_id(0)
    width = comb.shape[1]
    span = width // 2
    for half, three in (
        (0, ((own, own_c, 2), (down, down_c, 1), (sum_up, sum_up_c, 0))),
        (1, ((own, own_c, 3), (up, up_c, 1), (sum_down, sum_down_c, 0))),
    ):
        steps = [steps_of(tail[slot]) for _, tail, slot in three]
        for n in range(span // LANE):
            cols = slice(n * LANE, (n + 1) * LANE)
            a, b, c = [from_i16(r[slot, :, cols]) * s[n : n + 1] for (r, _, slot), s in zip(three, steps)]
            comb[:, half * span + n * LANE : half * span + (n + 1) * LANE] = a + b + c

    @pl.when(i == 3)
    def _():
        keep[...] = comb[...]

    for d, out in ((0, s1), (1, s2), (2, s3)):

        @pl.when(i == d)
        def _():
            codes[...] = jnp.zeros_like(codes)
            for n in range(width // LANE):
                cols = slice(n * LANE, (n + 1) * LANE)
                out[:, cols], codes[n : n + 1] = quantize(comb[:, cols])
            out[:, width:] = to_i16(codes[...])


def owner_chunk(y, pieces, after):
    span = pieces[0].shape[2] - PAD
    width = 2 * span
    row = lambda n, p: (((n + 1) & 3) ^ p[0], 0)
    full = lambda n, p: (0, 0)
    specs, ins = [], []
    for got in pieces:
        ins += [got, got]
        specs += [
            pl.BlockSpec((got.shape[0], QUARTER, span), lambda n, p: (0, ((n + 1) & 3) ^ p[0], 0)),
            pl.BlockSpec((got.shape[0], QUARTER, PAD), lambda n, p: (0, 0, span // PAD)),
        ]
    specs += [ANY] * len(after)
    shape = jax.ShapeDtypeStruct((QUARTER, width + PAD), I16)
    return pl.pallas_call(
        owner_kernel,
        grid_spec=pltpu.PrefetchScalarGridSpec(
            num_scalar_prefetch=1,
            grid=(4,),
            in_specs=specs,
            out_specs=[pl.BlockSpec((QUARTER, width), row), pl.BlockSpec((QUARTER, width), full)]
            + [pl.BlockSpec((QUARTER, width + PAD), full)] * 3,
            scratch_shapes=[pltpu.VMEM((QUARTER, PAD), F32)],
        ),
        out_shape=[
            jax.ShapeDtypeStruct((BLOCK, width), F32),
            jax.ShapeDtypeStruct((QUARTER, width), F32),
            shape,
            shape,
            shape,
        ],
        compiler_params=pltpu.CompilerParams(vmem_limit_bytes=16 << 20),
        cost_estimate=SMALL,
        name="sum_chips",
    )(y, *ins, *after)


def shard_kernel(width, count, *refs):
    ins, (out, codes) = refs[:count], refs[-2:]
    steps = [None if r.dtype == F32 else steps_of(r[:, width:]) for r in ins]
    codes[...] = jnp.zeros_like(codes)
    for n in range(width // LANE):
        cols = slice(n * LANE, (n + 1) * LANE)
        total = pair_sum(
            [r[:, cols] if s is None else from_i16(r[:, cols]) * s[n : n + 1] for r, s in zip(ins, steps)]
        )
        out[:, cols], codes[n : n + 1] = quantize(total)
    out[:, width:] = to_i16(codes[...])


def shard_sum(width, ins, after):
    rows = ins[0].shape[0]
    return pl.pallas_call(
        functools.partial(shard_kernel, width, len(ins)),
        in_specs=[VMEM] * len(ins) + [ANY] * len(after),
        out_specs=VMEM,
        out_shape=jax.ShapeDtypeStruct((rows, width + PAD), I16),
        scratch_shapes=[pltpu.VMEM((rows, PAD), F32)],
        compiler_params=pltpu.CompilerParams(vmem_limit_bytes=16 << 20),
        cost_estimate=SMALL,
        name="sum_replicas",
    )(*ins, *after)


def cast_sums(sums, q, mean):
    width = mean.shape[1]
    for d, s in enumerate(sums):
        step = steps_of(s[:, width:])
        row = pl.multiple_of((q ^ d) * QUARTER, QUARTER)
        for n in range(width // LANE):
            cols = slice(n * LANE, (n + 1) * LANE)
            mean[pl.ds(row, QUARTER), cols] = from_i16(s[:, cols]) * step[n : n + 1]


def factor_kernel(replicas, *refs):
    ranks, q, basis = refs[:3]
    sums, combs = (refs[3:7], refs[7:11]), refs[11:13]
    new_error, next_t, mean = refs[13:]
    row_at = lax.broadcasted_iota(jnp.int32, (8, 1), 0)
    tall = lax.broadcasted_iota(jnp.int32, (RANK_MAX, 1), 0)
    wide = lax.broadcasted_iota(jnp.int32, (1, RANK_MAX), 1)
    halves, grams, orthos, pivots = [], [], [], []
    for b in range(2):
        cast_sums(sums[b], q[0], mean)
        hi, lo = terms(mean[...])
        halves.append((hi, lo))
        rank = ranks[b]
        proj = dot(basis[b], hi, 1, 1) + dot(basis[b], lo, 1, 1)
        proj = jnp.where(tall < rank, proj, 0.0)
        gram = lax.dot_general(
            proj, proj, (((1,), (1,)), ((), ())), precision=lax.Precision.HIGHEST, preferred_element_type=F32
        )
        gram = jnp.where((tall < rank) & (wide < rank), gram, (tall == wide).astype(F32))
        grams.append([gram[8 * j : 8 * j + 8] for j in range(8)])
        orthos.append([proj[8 * j : 8 * j + 8] for j in range(8)])
        pivots.append([jnp.ones((8, 1), F32) for _ in range(8)])
    for k in range(RANK_MAX):
        at, own = divmod(k, 8)
        for gram, ortho, pivot in zip(grams, orthos, pivots):
            top = gram[at][own : own + 1, k : k + 1]
            pivot[at] = jnp.where(row_at == own, top, pivot[at])
            inverse = 1.0 / top
            top_g = gram[at][own : own + 1] * inverse
            top_o = ortho[at][own : own + 1] * inverse
            for j in range(at, 8):
                below = gram[j][:, k : k + 1]
                if j == at:
                    below = jnp.where(row_at > own, below, 0.0)
                gram[j] = gram[j] - below * top_g
                ortho[j] = ortho[j] - below * top_o
    for b in range(2):
        hi, lo = halves[b]
        scaled = [o * lax.rsqrt(p) for o, p in zip(orthos[b], pivots[b])]
        oh, ol = terms(jnp.concatenate(scaled, axis=0))
        back = (dot(oh, hi, 1, 0) + (dot(oh, lo, 1, 0) + dot(ol, hi, 1, 0))) * (1.0 / replicas)
        next_t[b] = back
        bh, bl = terms(back)
        approx = dot(oh, bh, 0, 0) + (dot(oh, bl, 0, 0) + dot(ol, bh, 0, 0))
        new_error[0, b * BLOCK : (b + 1) * BLOCK] = combs[b][...] - approx


def factor_blocks(ranks, q, basis_t, sums, combs, replicas):
    blocks, _, total = basis_t.shape
    return pl.pallas_call(
        functools.partial(factor_kernel, replicas),
        in_specs=[SMEM, SMEM] + [VMEM] * 11,
        out_specs=[VMEM, VMEM],
        out_shape=[
            jax.ShapeDtypeStruct((1, blocks * BLOCK, total), F32),
            jax.ShapeDtypeStruct((blocks, RANK_MAX, total), F32),
        ],
        scratch_shapes=[pltpu.VMEM((BLOCK, total), F32)],
        compiler_params=pltpu.CompilerParams(vmem_limit_bytes=40 << 20),
        cost_estimate=SMALL,
        name="factor",
    )(ranks, q, basis_t, *sums[0], *sums[1], *combs)


def per_device(hidden, out_grad, error_in, initial_basis, block_ranks):
    deep, wide = 8, 4
    replicas = deep * wide
    chips = 4
    g, r = lax.axis_index("grp"), lax.axis_index("rep")
    place = jnp.reshape(g, (1,)).astype(jnp.int32)
    z = r >> 2
    q = jnp.reshape(jnp.where((g & 1) == 0, r & 3, (z & 3) ^ (3 * (z >> 2))), (1,)).astype(jnp.int32)

    core_perm = [(x * 2 + c, x * 2 + 1 - c) for x in range(chips) for c in range(2)]

    def move(array, to):
        pairs = []
        for k in range(2 * chips):
            for z in range(deep):
                for i in range(wide):
                    z2, i2 = to(k & 1, z, i)
                    pairs.append((k * replicas + z * wide + i, k * replicas + (z2 % deep) * wide + i2 % wide))
        return lax.ppermute(array, ("grp", "rep"), pairs)

    def first(d):
        return lambda c, z, i: (z ^ d, i) if c else (z, i ^ d)

    def second(d):
        return lambda c, z, i: (z, i ^ d) if c else (z ^ d, i)

    og_sib = lax.ppermute(pick(place, out_grad), "grp", core_perm)
    h_sib = lax.ppermute(hidden, "grp", core_perm)

    def along_x(array, d):
        pairs = [(x * 2 + c, ((x + d) % chips) * 2 + c) for x in range(chips) for c in range(2)]
        return lax.ppermute(array, "grp", pairs)

    def start_x(block, after):
        up, down, keep = grad_chunk(place, out_grad, og_sib, hidden, h_sib, error_in, block, after)
        return keep, along_x(up, 1), along_x(down, -1)

    def add_x(pieces, after):
        up, down = relay(*pieces, after)
        return [*pieces, along_x(up, 1), along_x(down, -1)]

    def reduce_rows(pieces, after):
        comb, keep, *sends = owner_chunk(q, pieces, after)
        return comb, keep, [move(s, first(d)) for d, s in zip((1, 2, 3), sends)]

    def exchange(part):
        return [part] + [move(part, second(d)) for d in (1, 2, 3)]

    def pair(part):
        return [part, move(part, lambda c, z, i: (z ^ 7, i))]

    def gather(part):
        return [part] + [move(part, first(d)) for d in (1, 2, 3)]

    width = hidden.shape[1]
    basis_t = jnp.swapaxes(initial_basis, 1, 2)

    a = start_x(0, [])
    b = start_x(1, [a[0]])
    a = add_x(a, [b[0]])
    comb_a, keep_a, got_a = reduce_rows(a, [])
    b = add_x(b, [keep_a])
    comb_b, keep_b, got_b = reduce_rows(b, [])
    a1 = shard_sum(width, [keep_a, *got_a], [keep_b])
    b1 = shard_sum(width, [keep_b, *got_b], [a1])
    a2 = shard_sum(width, exchange(a1), [b1])
    b2 = shard_sum(width, exchange(b1), [a2])
    a3 = shard_sum(width, pair(a2), [b2])
    b3 = shard_sum(width, pair(b2), [a3])
    new_error, next_t = factor_blocks(
        block_ranks, q, basis_t, (gather(a3), gather(b3)), (comb_a, comb_b), replicas
    )
    return new_error, jnp.swapaxes(next_t, 1, 2)


def solution(mesh):
    return jax.shard_map(
        per_device,
        mesh=mesh,
        in_specs=(
            P(("grp", "rep"), None),
            P(("grp", "rep"), None),
            P("rep", "grp", None),
            P("grp", None, None),
            P("grp"),
        ),
        out_specs=(P("rep", "grp", None), P("grp", None, None)),
        check_vma=False,
    )
```

```python
import functools

import jax
import jax.numpy as jnp
from jax import lax
from jax.experimental import pallas as pl
from jax.experimental.pallas import tpu as pltpu
from jax.sharding import PartitionSpec as P

BLOCK = 128
RANK_MAX = 64
TILE = 256
LANE = 128
PAD = 128
F32 = jnp.float32
BF16 = jnp.bfloat16
I16 = jnp.int16
PEAK = 32767.0
SMALL = pl.CostEstimate(flops=1000, bytes_accessed=1000, transcendentals=0)
ANY = pl.BlockSpec(memory_space=pl.ANY)
VMEM = pl.BlockSpec(memory_space=pltpu.VMEM)
SMEM = pl.BlockSpec(memory_space=pltpu.SMEM)
FINE = 64.0


def code_of(top):
    return jnp.ceil(jnp.log2(jnp.maximum(top, 1e-30)) * FINE) + 1.0


def size_of(code):
    return jnp.exp2(code * (1.0 / FINE))


def to_i16(x):
    return x.astype(jnp.int32).astype(I16)


def from_i16(x):
    return x.astype(jnp.int32).astype(F32)


def quantize(x):
    code = code_of(jnp.max(jnp.abs(x), axis=0, keepdims=True))
    return to_i16(jnp.round(x * (PEAK / size_of(code)))), code


def steps_of(codes):
    return size_of(from_i16(codes)) * (1.0 / PEAK)


def terms(x):
    hi = x.astype(BF16)
    rest = x - hi.astype(F32)
    return hi, rest.astype(BF16)


def dot(a, b, ca, cb):
    return lax.dot_general(a, b, (((ca,), (cb,)), ((), ())), preferred_element_type=F32)


def dot3(a, b, ca, cb):
    ah, al = terms(a)
    bh, bl = terms(b)
    return dot(ah, bh, ca, cb) + (dot(ah, bl, ca, cb) + dot(al, bh, ca, cb))


def grad_kernel(place, *refs):
    own, sib, (h, h_sib, err) = refs[:4], refs[4:8], refs[8:11]
    up, down, keep, lhs, codes = refs[-5:]
    half = pl.program_id(0)
    tok, span = h.shape

    @pl.when(half == 0)
    def _():
        for k in range(4):
            rows = slice(k * BLOCK, (k + 1) * BLOCK)
            lhs[rows, :tok] = own[k][...].T
            lhs[rows, tok:] = sib[k][...].T
        codes[...] = jnp.zeros_like(codes)

    def work(slots):
        left, right = lhs[:, :tok], lhs[:, tok:]
        for at in range(0, span, TILE):
            size = min(TILE, span - at)
            cols = slice(at, at + size)
            total = dot(left, h[:, cols], 1, 0) + dot(right, h_sib[:, cols], 1, 0)
            for k, (out, slot) in enumerate(slots):
                part = total[k * BLOCK : (k + 1) * BLOCK]
                if k == 0:
                    part += err[0, :, cols].astype(F32)
                out[slot, :, cols], code = quantize(part)
                for i in range(size // LANE):
                    codes[k, at // LANE + i : at // LANE + i + 1] = code[:, i * LANE : (i + 1) * LANE]
        for k, (out, slot) in enumerate(slots):
            out[slot, :, span:] = to_i16(codes[k])

    @pl.when(half == 0)
    def _():
        work(((keep, 2), (keep, 0), (up, 0), (down, 1)))

    @pl.when(half == 1)
    def _():
        work(((keep, 3), (up, 1), (down, 0), (keep, 1)))


def grad_chunk(place, og, og_sib, h, h_sib, err, block, after):
    tok = og.shape[0]
    span = h.shape[1] // 2
    fixed = lambda n, p: (0, 0, 0)

    def own(k):
        return pl.BlockSpec((tok, BLOCK), lambda n, p: (0, (((p[0] >> 1) + k) & 3) * 4 + (p[0] & 1) * 2 + block))

    def sib(k):
        return pl.BlockSpec((tok, BLOCK), lambda n, p: (0, (((p[0] >> 1) + k) & 3) * 2 + block))

    return pl.pallas_call(
        grad_kernel,
        grid_spec=pltpu.PrefetchScalarGridSpec(
            num_scalar_prefetch=1,
            grid=(2,),
            in_specs=[
                *[own(k) for k in range(4)],
                *[sib(k) for k in range(4)],
                pl.BlockSpec((tok, span), lambda n, p: (0, n)),
                pl.BlockSpec((tok, span), lambda n, p: (0, n)),
                pl.BlockSpec((1, BLOCK, span), lambda n, p: (0, block, n)),
            ]
            + [ANY] * len(after),
            out_specs=[pl.BlockSpec((n, BLOCK, span + PAD), fixed) for n in (2, 2, 4)],
            scratch_shapes=[
                pltpu.VMEM((4 * BLOCK, 2 * tok), BF16),
                pltpu.VMEM((4, BLOCK, PAD), F32),
            ],
        ),
        out_shape=[jax.ShapeDtypeStruct((n, BLOCK, span + PAD), I16) for n in (2, 2, 4)],
        compiler_params=pltpu.CompilerParams(vmem_limit_bytes=60 << 20),
        cost_estimate=SMALL,
        name="chip_gradient",
    )(place, *[og] * 4, *[og_sib] * 4, h, h_sib, err, *after)


def relay_kernel(keep, got_up, got_down, *refs):
    up, down, codes = refs[-3:]
    span = up.shape[2] - PAD
    codes[...] = jnp.zeros_like(codes)
    for slot, got, out in ((0, got_up, up), (1, got_down, down)):
        mine, others = steps_of(keep[slot, :QUARTER, span:]), steps_of(got[0, :QUARTER, span:])
        for n in range(span // LANE):
            cols = slice(n * LANE, (n + 1) * LANE)
            total = from_i16(keep[slot, :, cols]) * mine[n : n + 1] + from_i16(got[0, :, cols]) * others[n : n + 1]
            out[0, :, cols], codes[n : n + 1] = quantize(total)
        out[0, :, span:] = to_i16(codes[...])


def relay(keep, got_up, got_down, after):
    wide = keep.shape[2]
    fixed = lambda n: (0, 0, 0)
    one = pl.BlockSpec((1, BLOCK, wide), fixed)
    return pl.pallas_call(
        relay_kernel,
        grid=(1,),
        in_specs=[pl.BlockSpec((2, BLOCK, wide), fixed), one, one] + [ANY] * len(after),
        out_specs=[one, one],
        out_shape=[jax.ShapeDtypeStruct((1, BLOCK, wide), I16)] * 2,
        scratch_shapes=[pltpu.VMEM((BLOCK, PAD), F32)],
        compiler_params=pltpu.CompilerParams(vmem_limit_bytes=16 << 20),
        cost_estimate=SMALL,
        name="add_on_the_way",
    )(keep, got_up, got_down, *after)


def pick_kernel(place, og, out):
    out[...] = og[...]


def pick(place, og):
    tok, rows = og.shape
    return pl.pallas_call(
        pick_kernel,
        grid_spec=pltpu.PrefetchScalarGridSpec(
            num_scalar_prefetch=1,
            grid=(4,),
            in_specs=[pl.BlockSpec((tok, 256), lambda n, p: (0, n * 2 + 1 - (p[0] & 1)))],
            out_specs=pl.BlockSpec((tok, 256), lambda n, p: (0, n)),
        ),
        out_shape=jax.ShapeDtypeStruct((tok, rows // 2), BF16),
        name="pick_columns",
    )(place, og)


QUARTER = BLOCK // 4


def pair_sum(parts):
    while len(parts) > 1:
        half = len(parts) // 2
        parts = [parts[i] + parts[i + half] for i in range(half)]
    return parts[0]


def owner_kernel(place, *refs):
    (comb, keep, s1, s2, s3, codes) = refs[-6:]
    own, own_c, up, up_c, down, down_c, sum_up, sum_up_c, sum_down, sum_down_c = refs[:10]
    i = pl.program_id(0)
    width = comb.shape[1]
    span = width // 2
    for half, three in (
        (0, ((own, own_c, 2), (down, down_c, 1), (sum_up, sum_up_c, 0))),
        (1, ((own, own_c, 3), (up, up_c, 1), (sum_down, sum_down_c, 0))),
    ):
        steps = [steps_of(tail[slot]) for _, tail, slot in three]
        for n in range(span // LANE):
            cols = slice(n * LANE, (n + 1) * LANE)
            a, b, c = [from_i16(r[slot, :, cols]) * s[n : n + 1] for (r, _, slot), s in zip(three, steps)]
            comb[:, half * span + n * LANE : half * span + (n + 1) * LANE] = a + b + c

    @pl.when(i == 3)
    def _():
        keep[...] = comb[...]

    for d, out in ((0, s1), (1, s2), (2, s3)):

        @pl.when(i == d)
        def _():
            codes[...] = jnp.zeros_like(codes)
            for n in range(width // LANE):
                cols = slice(n * LANE, (n + 1) * LANE)
                out[:, cols], codes[n : n + 1] = quantize(comb[:, cols])
            out[:, width:] = to_i16(codes[...])


def owner_chunk(y, pieces, after):
    span = pieces[0].shape[2] - PAD
    width = 2 * span
    row = lambda n, p: (((n + 1) & 3) ^ p[0], 0)
    full = lambda n, p: (0, 0)
    specs, ins = [], []
    for got in pieces:
        ins += [got, got]
        specs += [
            pl.BlockSpec((got.shape[0], QUARTER, span), lambda n, p: (0, ((n + 1) & 3) ^ p[0], 0)),
            pl.BlockSpec((got.shape[0], QUARTER, PAD), lambda n, p: (0, 0, span // PAD)),
        ]
    specs += [ANY] * len(after)
    shape = jax.ShapeDtypeStruct((QUARTER, width + PAD), I16)
    return pl.pallas_call(
        owner_kernel,
        grid_spec=pltpu.PrefetchScalarGridSpec(
            num_scalar_prefetch=1,
            grid=(4,),
            in_specs=specs,
            out_specs=[pl.BlockSpec((QUARTER, width), row), pl.BlockSpec((QUARTER, width), full)]
            + [pl.BlockSpec((QUARTER, width + PAD), full)] * 3,
            scratch_shapes=[pltpu.VMEM((QUARTER, PAD), F32)],
        ),
        out_shape=[
            jax.ShapeDtypeStruct((BLOCK, width), F32),
            jax.ShapeDtypeStruct((QUARTER, width), F32),
            shape,
            shape,
            shape,
        ],
        compiler_params=pltpu.CompilerParams(vmem_limit_bytes=16 << 20),
        cost_estimate=SMALL,
        name="sum_chips",
    )(y, *ins, *after)


def shard_kernel(width, count, *refs):
    ins, (out, codes) = refs[:count], refs[-2:]
    steps = [None if r.dtype == F32 else steps_of(r[:, width:]) for r in ins]
    codes[...] = jnp.zeros_like(codes)
    for n in range(width // LANE):
        cols = slice(n * LANE, (n + 1) * LANE)
        total = pair_sum(
            [r[:, cols] if s is None else from_i16(r[:, cols]) * s[n : n + 1] for r, s in zip(ins, steps)]
        )
        out[:, cols], codes[n : n + 1] = quantize(total)
    out[:, width:] = to_i16(codes[...])


def shard_sum(width, ins, after):
    rows = ins[0].shape[0]
    return pl.pallas_call(
        functools.partial(shard_kernel, width, len(ins)),
        in_specs=[VMEM] * len(ins) + [ANY] * len(after),
        out_specs=VMEM,
        out_shape=jax.ShapeDtypeStruct((rows, width + PAD), I16),
        scratch_shapes=[pltpu.VMEM((rows, PAD), F32)],
        compiler_params=pltpu.CompilerParams(vmem_limit_bytes=16 << 20),
        cost_estimate=SMALL,
        name="sum_replicas",
    )(*ins, *after)


def cast_sums(sums, q, mean):
    width = mean.shape[1]
    for d, s in enumerate(sums):
        step = steps_of(s[:, width:])
        row = pl.multiple_of((q ^ d) * QUARTER, QUARTER)
        for n in range(width // LANE):
            cols = slice(n * LANE, (n + 1) * LANE)
            mean[pl.ds(row, QUARTER), cols] = from_i16(s[:, cols]) * step[n : n + 1]


def factor_kernel(replicas, *refs):
    ranks, q, basis = refs[:3]
    sums, combs = (refs[3:7], refs[7:11]), refs[11:13]
    new_error, next_t, mean = refs[13:]
    row_at = lax.broadcasted_iota(jnp.int32, (8, 1), 0)
    tall = lax.broadcasted_iota(jnp.int32, (RANK_MAX, 1), 0)
    wide = lax.broadcasted_iota(jnp.int32, (1, RANK_MAX), 1)
    halves, grams, orthos, pivots = [], [], [], []
    for b in range(2):
        cast_sums(sums[b], q[0], mean)
        hi, lo = terms(mean[...])
        halves.append((hi, lo))
        rank = ranks[b]
        proj = dot(basis[b], hi, 1, 1) + dot(basis[b], lo, 1, 1)
        proj = jnp.where(tall < rank, proj, 0.0)
        gram = lax.dot_general(
            proj, proj, (((1,), (1,)), ((), ())), precision=lax.Precision.HIGHEST, preferred_element_type=F32
        )
        gram = jnp.where((tall < rank) & (wide < rank), gram, (tall == wide).astype(F32))
        grams.append([gram[8 * j : 8 * j + 8] for j in range(8)])
        orthos.append([proj[8 * j : 8 * j + 8] for j in range(8)])
        pivots.append([jnp.ones((8, 1), F32) for _ in range(8)])
    for k in range(RANK_MAX):
        at, own = divmod(k, 8)
        for gram, ortho, pivot in zip(grams, orthos, pivots):
            top = gram[at][own : own + 1, k : k + 1]
            pivot[at] = jnp.where(row_at == own, top, pivot[at])
            inverse = 1.0 / top
            top_g = gram[at][own : own + 1] * inverse
            top_o = ortho[at][own : own + 1] * inverse
            for j in range(at, 8):
                below = gram[j][:, k : k + 1]
                if j == at:
                    below = jnp.where(row_at > own, below, 0.0)
                gram[j] = gram[j] - below * top_g
                ortho[j] = ortho[j] - below * top_o
    for b in range(2):
        hi, lo = halves[b]
        scaled = [o * lax.rsqrt(p) for o, p in zip(orthos[b], pivots[b])]
        oh, ol = terms(jnp.concatenate(scaled, axis=0))
        back = (dot(oh, hi, 1, 0) + (dot(oh, lo, 1, 0) + dot(ol, hi, 1, 0))) * (1.0 / replicas)
        next_t[b] = back
        bh, bl = terms(back)
        approx = dot(oh, bh, 0, 0) + (dot(oh, bl, 0, 0) + dot(ol, bh, 0, 0))
        new_error[0, b * BLOCK : (b + 1) * BLOCK] = combs[b][...] - approx


def factor_blocks(ranks, q, basis_t, sums, combs, replicas):
    blocks, _, total = basis_t.shape
    return pl.pallas_call(
        functools.partial(factor_kernel, replicas),
        in_specs=[SMEM, SMEM] + [VMEM] * 11,
        out_specs=[VMEM, VMEM],
        out_shape=[
            jax.ShapeDtypeStruct((1, blocks * BLOCK, total), F32),
            jax.ShapeDtypeStruct((blocks, RANK_MAX, total), F32),
        ],
        scratch_shapes=[pltpu.VMEM((BLOCK, total), F32)],
        compiler_params=pltpu.CompilerParams(vmem_limit_bytes=40 << 20),
        cost_estimate=SMALL,
        name="factor",
    )(ranks, q, basis_t, *sums[0], *sums[1], *combs)


def per_device(hidden, out_grad, error_in, initial_basis, block_ranks):
    deep, wide = 8, 4
    replicas = deep * wide
    chips = 4
    g, r = lax.axis_index("grp"), lax.axis_index("rep")
    place = jnp.reshape(g, (1,)).astype(jnp.int32)
    z = r >> 2
    q = jnp.reshape(jnp.where((g & 1) == 0, r & 3, (z & 3) ^ (3 * (z >> 2))), (1,)).astype(jnp.int32)

    core_perm = [(x * 2 + c, x * 2 + 1 - c) for x in range(chips) for c in range(2)]

    def move(array, to):
        pairs = []
        for k in range(2 * chips):
            for z in range(deep):
                for i in range(wide):
                    z2, i2 = to(k & 1, z, i)
                    pairs.append((k * replicas + z * wide + i, k * replicas + (z2 % deep) * wide + i2 % wide))
        return lax.ppermute(array, ("grp", "rep"), pairs)

    def first(d):
        return lambda c, z, i: (z ^ d, i) if c else (z, i ^ d)

    def second(d):
        return lambda c, z, i: (z, i ^ d) if c else (z ^ d, i)

    og_sib = lax.ppermute(pick(place, out_grad), "grp", core_perm)
    h_sib = lax.ppermute(hidden, "grp", core_perm)

    def along_x(array, d):
        pairs = [(x * 2 + c, ((x + d) % chips) * 2 + c) for x in range(chips) for c in range(2)]
        return lax.ppermute(array, "grp", pairs)

    def start_x(block, after):
        up, down, keep = grad_chunk(place, out_grad, og_sib, hidden, h_sib, error_in, block, after)
        return keep, along_x(up, 1), along_x(down, -1)

    def add_x(pieces, after):
        up, down = relay(*pieces, after)
        return [*pieces, along_x(up, 1), along_x(down, -1)]

    def reduce_rows(pieces, after):
        comb, keep, *sends = owner_chunk(q, pieces, after)
        return comb, keep, [move(s, first(d)) for d, s in zip((1, 2, 3), sends)]

    def exchange(part):
        return [part] + [move(part, second(d)) for d in (1, 2, 3)]

    def pair(part):
        return [part, move(part, lambda c, z, i: (z ^ 7, i))]

    def gather(part):
        return [part] + [move(part, first(d)) for d in (1, 2, 3)]

    width = hidden.shape[1]
    basis_t = jnp.swapaxes(initial_basis, 1, 2)

    a = start_x(0, [])
    b = start_x(1, [a[0]])
    a = add_x(a, [b[0]])
    comb_a, keep_a, got_a = reduce_rows(a, [])
    b = add_x(b, [keep_a])
    comb_b, keep_b, got_b = reduce_rows(b, [])
    a1 = shard_sum(width, [keep_a, *got_a], [keep_b])
    b1 = shard_sum(width, [keep_b, *got_b], [a1])
    a2 = shard_sum(width, exchange(a1), [b1])
    b2 = shard_sum(width, exchange(b1), [a2])
    a3 = shard_sum(width, pair(a2), [b2])
    b3 = shard_sum(width, pair(b2), [a3])
    new_error, next_t = factor_blocks(
        block_ranks, q, basis_t, (gather(a3), gather(b3)), (comb_a, comb_b), replicas
    )
    return new_error, jnp.swapaxes(next_t, 1, 2)


def solution(mesh):
    return jax.shard_map(
        per_device,
        mesh=mesh,
        in_specs=(
            P(("grp", "rep"), None),
            P(("grp", "rep"), None),
            P("rep", "grp", None),
            P("grp", None, None),
            P("grp"),
        ),
        out_specs=(P("rep", "grp", None), P("grp", None, None)),
        check_vma=False,
    )
```
